32 devices in a mesh: groups: 2 (over x), dp: 16 (over z, y, core).
Axes of the slice: x: 2, y: 2, z: 4, core: 2. Of those that a mesh axis runs over, the one named last changes fastest.
Arguments:
- queries: bfloat16 [24576, 4096], P(('groups', 'dp')), parts along dimension 0, may hold values from -120 to 120
- keys: bfloat16 [24576, 512], P(('groups', 'dp')), parts along dimension 0, may hold values from -6 to 6
- values: bfloat16 [24576, 512], P(('groups', 'dp')), parts along dimension 0, may hold values from -6 to 6
- block_counts: int32 [32], P(('groups', 'dp')), parts along dimension 0, may hold values from 0 to 6, as said below
- segment_ids: int32 [8192], P(('groups', 'dp')), parts along dimension 0, may hold values from 0 to 7, never falling along the last dimension, each value on 1 to 1024 neighbouring positions
- reward_dir: float32 [4096], replicated, may hold values from -4 to 4
Outputs:
- attn_out: bfloat16 [8192, 4096], P(('groups', 'dp')), parts along dimension 0
- rewards: float32 [16], P('groups'), parts along dimension 0
The draws below stay inside these ranges and needn't reach their ends.
There are 2 independent parts, one for each index of `groups`. The reference program is written for one: setup_inputs(seed, part) draws one part's arguments, and reference() takes and returns one part's arrays. A program takes and returns all parts, laid end to end along the dimension named above; an argument that names none is the same for every part. Nothing has to cross between parts.
Inputs may be any that keep to these rules, and one draw needn't show every extreme that they name: `block_counts`: the counts sum to 2 times the number of ranks; for each rank s the counts of the ranks before s sum to between (2 * s - 2) and (2 * s + 2); some rank holds 6. `segment_ids`: positions never fall in segment number, each of the 8 responses holds 1 to 1024 positions.
All inputs are finite; a program needn't handle non-finite values.
Results may differ from the reference program's by a relative error of at most 0.0039.
The reference program's roundings to bfloat16 on the way (of `soft_weights`) count: a program that leaves them out, or rounds other values in their place, can miss the bound.
Values may be sent and summed in bfloat16 or wider, within the bound.
A program may use at most 128 MiB of HBM per device.

```python
import math
import jax
import jax.numpy as jnp
import numpy as np
from jax import lax

D_HEAD = 128
HEADS = 32
KV_HEADS = 4
BLOCK = 128
RECV = 2
REACH = 4
CAP = 6
TOKENS = 4096
SRC_TOK = 12288
MAXLEN = 1024
NRESP = 8
N_DP = 16


def pair_draw(key):
    query_key = jax.random.fold_in(key, 11)
    key_key = jax.random.fold_in(key, 12)
    key_rows = jnp.clip(jax.random.normal(key_key, (SRC_TOK, KV_HEADS * D_HEAD), jnp.float32), -6.0, 6.0)
    query_rows = jnp.clip(jax.random.normal(query_key, (SRC_TOK, HEADS * D_HEAD), jnp.float32), -6.0, 6.0)
    return (query_rows, key_rows)


def draw_queries(key, part):
    return pair_draw(key)[0].astype(jnp.bfloat16)


def draw_keys(key, part):
    return pair_draw(key)[1].astype(jnp.bfloat16)


def draw_block_counts(key, part):
    marker = jnp.arange(N_DP + 1, dtype=jnp.int32)
    peak_rank = jax.random.randint(jax.random.fold_in(key, 22), (), 2, N_DP - 2).astype(jnp.int32)
    peak_rank = jnp.where(peak_rank >= N_DP // 2, peak_rank + 1, peak_rank).astype(jnp.int32)
    turn_rank = jax.random.randint(jax.random.fold_in(key, 23), (), 0, peak_rank - 1).astype(jnp.int32)
    excess = jnp.zeros((N_DP + 1,), jnp.int32)
    excess = jnp.where((marker >= 1) & (marker <= turn_rank), RECV, excess)
    excess = jnp.where((marker >= turn_rank + 2) & (marker <= peak_rank), -RECV, excess)
    excess = jnp.where((marker >= peak_rank + 1) & (marker <= N_DP - 1), RECV, excess)
    return (RECV + excess[1:] - excess[:-1]).astype(jnp.int32)


def block_levels(own_key, dims, cuts, least, high):
    factor_of = 1.0
    for position, parts in cuts:
        draws = jax.random.uniform(jax.random.fold_in(jax.random.fold_in(own_key, 6), position), (parts,), jnp.float32, least / len(cuts), high / len(cuts))
        factor_of = factor_of * jnp.repeat(jnp.exp(draws), dims[position] // parts).reshape((-1,) + (1,) * (len(dims) - 1 - position))
    return factor_of


def profile(amount, total, most, lean):
    loads = [(1 << 20) // math.isqrt(standing ** lean) + 1 for standing in range(2, amount + 1)]
    surplus, given = total - most - (amount - 1), [1] * (amount - 1)
    while surplus > 0:
        movable = [i for i in range(amount - 1) if given[i] < most]
        mass, budget = sum([loads[i] for i in movable]), surplus
        for i in movable:
            addition = min(most - given[i], max(1, budget * loads[i] // mass), surplus)
            given[i] = given[i] + addition
            surplus = surplus - addition
    return np.array([most] + given)


def ragged_sizes(own_key, number_of, total, most, skew):
    if number_of == 2:
        one = jax.random.randint(own_key, (), max(1, total - most), min(most, total - 1) + 1)
        return jnp.stack([one, total - one])
    sizes = jnp.asarray(profile(number_of, total, most, skew), jnp.int32)
    twos = (number_of - 1) // 2
    giver, taker = sizes[1:1 + 2 * twos:2], sizes[2:2 + 2 * twos:2]
    margin = jnp.minimum(giver - 1, most - taker)
    passed = jax.random.randint(jax.random.fold_in(own_key, 1), (twos,), 0, 1 << 20) % (margin + 1)
    sizes = sizes.at[1:1 + 2 * twos:2].set(giver - passed).at[2:2 + 2 * twos:2].set(taker + passed)
    return sizes[jax.random.permutation(jax.random.fold_in(own_key, 2), number_of)]


def bell_draw(rng, extent, spread, most, shards=(), held_as=jnp.bfloat16):
    result = spread * jax.random.normal(rng, extent, jnp.float32)
    if shards:
        result = result * block_levels(rng, extent, shards, -0.22, 0.18)
    return jnp.clip(result, -most, most).astype(held_as)


def setup_inputs(seed: int = 0, part: int = 0) -> dict:
    key_of = jax.random.split(jax.random.key(seed), 7)
    part_splits = jax.random.split(jax.random.fold_in(key_of[6], part), 7)
    queries = draw_queries(jax.random.fold_in(jax.random.fold_in(key_of[6], part), 71), part)
    keys = draw_keys(jax.random.fold_in(jax.random.fold_in(key_of[6], part), 71), part)
    values = bell_draw(part_splits[2], (SRC_TOK, KV_HEADS * D_HEAD), 1.0, 6.0, ((0, 16),))
    block_counts = draw_block_counts(jax.random.fold_in(jax.random.fold_in(key_of[6], part), 71), part)
    segment_ids = jnp.searchsorted(jnp.cumsum(ragged_sizes(part_splits[4], NRESP, TOKENS, MAXLEN, 1)), jnp.arange(TOKENS), side="right").astype(jnp.int32)
    reward_dir = bell_draw(key_of[5], (HEADS * D_HEAD,), 0.25, 4.0, (), jnp.float32)
    return {"queries": queries, "keys": keys, "values": values, "block_counts": block_counts, "segment_ids": segment_ids, "reward_dir": reward_dir}


def attend(query_rows, key_window, value_window, allowed):
    per_group = HEADS // KV_HEADS
    row_count = query_rows.shape[0]
    score_scale = D_HEAD ** -0.5
    grouped = query_rows.reshape(row_count, KV_HEADS, per_group, D_HEAD)
    key_heads = key_window.reshape(-1, KV_HEADS, D_HEAD)
    value_heads = value_window.reshape(-1, KV_HEADS, D_HEAD)
    head_outs = []
    for head_index in range(KV_HEADS):
        query_head = grouped[:, head_index].reshape(row_count * per_group, D_HEAD)
        logits = jnp.dot(query_head, key_heads[:, head_index].T, preferred_element_type=jnp.float32) * score_scale
        logits = logits.reshape(row_count, per_group, -1)
        logits = jnp.where(allowed[:, None, :], logits, -1e30)
        row_max = jnp.max(logits, axis=-1, keepdims=True)
        raised = jnp.exp(logits - row_max)
        totals = jnp.sum(raised, axis=-1)
        soft_weights = raised.astype(jnp.bfloat16).reshape(row_count * per_group, -1)
        head_out = jnp.dot(soft_weights, value_heads[:, head_index], preferred_element_type=jnp.float32)
        head_out = head_out.reshape(row_count, per_group, D_HEAD) / totals[..., None]
        head_outs.append(head_out.astype(jnp.bfloat16))
    return jnp.stack(head_outs, axis=1).reshape(row_count, HEADS * D_HEAD)


def reference(queries, keys, values, block_counts, segment_ids, reward_dir):
    row_count = RECV * BLOCK
    offsets = (jnp.cumsum(block_counts) - block_counts).astype(jnp.int32)
    slot_index = jnp.arange(CAP, dtype=jnp.int32)
    target = offsets[:, None] + slot_index[None, :]
    target = jnp.where(slot_index[None, :] < block_counts[:, None], target, N_DP * RECV).reshape(-1)

    def arrange(source):
        blocks = source.reshape(N_DP * CAP, BLOCK, source.shape[1])
        placed = jnp.zeros((N_DP * RECV, BLOCK, source.shape[1]), source.dtype)
        placed = placed.at[target].set(blocks, mode="drop")
        return placed.reshape(N_DP * RECV * BLOCK, source.shape[1])

    packed_queries = arrange(queries)
    packed_keys = arrange(keys)
    packed_values = arrange(values)
    positions = jnp.arange(TOKENS, dtype=jnp.int32)
    changed = jnp.concatenate([jnp.ones((1,), bool), segment_ids[1:] != segment_ids[:-1]])
    starts = lax.cummax(jnp.where(changed, positions, 0).astype(jnp.int32), axis=0)
    is_last = jnp.concatenate([segment_ids[1:] != segment_ids[:-1], jnp.ones((1,), bool)])
    reach_rows = REACH * row_count
    padded_keys = jnp.concatenate([jnp.zeros((reach_rows, packed_keys.shape[1]), jnp.bfloat16), packed_keys])
    padded_values = jnp.concatenate([jnp.zeros((reach_rows, packed_values.shape[1]), jnp.bfloat16), packed_values])

    def one_block(block_index):
        row_start = (block_index * row_count).astype(jnp.int32)
        query_rows = lax.dynamic_slice_in_dim(packed_queries, row_start, row_count, 0)
        key_window = lax.dynamic_slice_in_dim(padded_keys, row_start, reach_rows + row_count, 0)
        value_window = lax.dynamic_slice_in_dim(padded_values, row_start, reach_rows + row_count, 0)
        key_pos = row_start - reach_rows + jnp.arange(reach_rows + row_count, dtype=jnp.int32)
        query_pos = row_start + jnp.arange(row_count, dtype=jnp.int32)
        query_starts = lax.dynamic_slice_in_dim(starts, row_start, row_count, 0)
        allowed = (key_pos[None, :] >= query_starts[:, None]) & (key_pos[None, :] <= query_pos[:, None])
        return attend(query_rows, key_window, value_window, allowed)

    attn_out = lax.map(one_block, jnp.arange(N_DP, dtype=jnp.int32)).reshape(TOKENS, HEADS * D_HEAD)
    token_score = jnp.dot(attn_out.astype(jnp.float32), reward_dir, precision=lax.Precision.HIGHEST)
    rewards = jnp.zeros((NRESP,), jnp.float32).at[segment_ids].add(jnp.where(is_last, token_score, 0.0))
    return attn_out, rewards
```

```python
import functools

import jax
import jax.numpy as jnp
from jax import lax
from jax.experimental import pallas as pl
from jax.experimental.pallas import tpu as pltpu
from jax.sharding import PartitionSpec as P

D_HEAD = 128
HEADS = 32
KV_HEADS = 4
BLOCK = 128
REACH = 4
LANES = 128
PER_GROUP = HEADS // KV_HEADS
LOG2E = 1.4426950408889634
MASKED = -1e30


def kernel(
    n, q_hbm, k_hbm, v_hbm, meta_ref, cols_ref, dir_ref, out_ref, rew_ref,
    qv, kv, vv, meta_all, send_q, recv_q, send_kv, recv_kv, win, qp, bias, score,
    part, part_all,
    load_sem, meta_send, meta_recv, kv_send, kv_recv, q_send, q_recv,
    win_send, win_recv, part_send, part_recv,
):
    me = lax.axis_index("dp")
    core = lax.rem(me, 2)
    partner = me + 1 - 2 * core
    rows = cols_ref.shape[1]
    recv = rows // BLOCK
    cap = qv.shape[0]
    width = PER_GROUP * D_HEAD
    kv_width = KV_HEADS * D_HEAD
    id_rows = rows // LANES

    loads = [
        pltpu.make_async_copy(k_hbm, kv, load_sem.at[0]),
        pltpu.make_async_copy(v_hbm, vv, load_sem.at[1]),
        pltpu.make_async_copy(q_hbm, qv, load_sem.at[2]),
    ]
    for load in loads:
        load.start()

    for pad in list(range(REACH)) + [n + REACH]:
        meta_all[pad] = jnp.full((8, LANES), -1, jnp.int32)
    meta_all[pl.ds(me + REACH, 1)] = meta_ref[...][None]
    for distance in (2, 4):
        @pl.when(me < distance)
        def _():
            win[:, pl.ds((4 - distance) * rows, 2 * rows), :] = jnp.zeros(
                (KV_HEADS, 2 * rows, 2 * D_HEAD), win.dtype
            )
    score[...] = jnp.zeros_like(score)

    barrier = pltpu.get_barrier_semaphore()

    def greet(i, carry):
        pl.semaphore_signal(
            barrier, inc=1, device_id={"dp": lax.rem(me + i, n)},
            device_id_type=pl.DeviceIdType.MESH,
        )
        return carry

    lax.fori_loop(1, n, greet, 0)
    pl.semaphore_wait(barrier, n - 1)

    def remote(src, dst, send_sem, recv_sem, rank):
        return pltpu.make_async_remote_copy(
            src_ref=src, dst_ref=dst, send_sem=send_sem, recv_sem=recv_sem,
            device_id={"dp": rank}, device_id_type=pl.DeviceIdType.MESH,
        )

    def tell_all(src, table, shift, send_sem, recv_sem):
        def begin(i, carry):
            remote(src, table.at[me + shift], send_sem.at[i], recv_sem.at[i],
                   lax.rem(me + i, n)).start()
            return carry

        lax.fori_loop(1, n, begin, 0)

    def hear_all(src, table, shift, send_sem, recv_sem):
        def finish(i, carry):
            came = lax.rem(me + n - i, n)
            remote(src, table.at[came + shift], send_sem.at[i], recv_sem.at[i],
                   lax.rem(me + i, n)).wait()
            return carry

        lax.fori_loop(1, n, finish, 0)

    tell_all(meta_ref, meta_all, REACH, meta_send, meta_recv)
    hear_all(meta_ref, meta_all, REACH, meta_send, meta_recv)

    counts = meta_all[REACH:REACH + n, id_rows, :]
    rank_index = lax.broadcasted_iota(jnp.int32, (n, LANES), 0)
    offset = jnp.sum(jnp.where(rank_index < me, counts, 0), axis=0, keepdims=True)[0, 0]
    count = meta_ref[id_rows:id_rows + 1, :][0, 0]

    def pick(distance, slot):
        return jnp.clip((me + distance) * recv + slot - offset, 0, cap - 1)

    routes = ((0, 1, me + 1, me < n - 1, me > 0), (1, -1, me - 1, me > 0, me < n - 1))

    def both(start_or_wait):
        for d, distance, rank, sends, receives in routes:
            start_or_wait(d, rank, sends, receives)

    for load in loads[:2]:
        load.wait()
    for d, distance, rank, sends, receives in routes:
        for slot in range(recv):
            at = pl.ds(slot * BLOCK, BLOCK)
            chosen = pick(distance, slot)
            send_kv[d, at, :kv_width] = kv[chosen]
            send_kv[d, at, kv_width:] = vv[chosen]

        @pl.when(sends)
        def _():
            remote(send_kv.at[d], recv_kv.at[d], kv_send.at[d], kv_recv.at[d], rank).start()

    loads[2].wait()

    def prepare_q(g):
        for d, distance, rank, sends, receives in routes:
            for slot in range(recv):
                send_q[d, g, pl.ds(slot * BLOCK, BLOCK), :] = qv[
                    pick(distance, slot), :, g * width:(g + 1) * width
                ]

    def q_copy(d, g, rank):
        return remote(send_q.at[d, g], recv_q.at[d, g], q_send.at[d, g], q_recv.at[d, g], rank)

    def start_q(g):
        for d, distance, rank, sends, receives in routes:
            @pl.when(sends)
            def _():
                q_copy(d, g, rank).start()

    prepare_q(0)
    start_q(0)
    prepare_q(1)

    row_at = lax.broadcasted_iota(jnp.int32, (rows, LANES), 0)
    lane_at = lax.broadcasted_iota(jnp.int32, (rows, LANES), 1)
    ids = cols_ref[0]
    for chunk in range((REACH + 1) * id_rows):
        key_ids = meta_all[pl.ds(me + chunk // id_rows, 1)][0, chunk % id_rows:chunk % id_rows + 1, :]
        key_at = lane_at + (chunk * LANES - REACH * rows)
        bias[:, chunk * LANES:(chunk + 1) * LANES] = jnp.where(
            (ids == key_ids) & (key_at <= row_at), 0.0, MASKED
        )

    for d, distance, rank, sends, receives in routes:
        @pl.when(receives)
        def _():
            remote(send_kv.at[d], recv_kv.at[d], kv_send.at[d], kv_recv.at[d], rank).wait_recv()

    def source(slot):
        block = me * recv + slot
        return block < offset, block >= offset + count

    for slot in range(recv):
        before, after = source(slot)
        at = pl.ds(slot * BLOCK, BLOCK)
        home = pl.ds((4 + core) * rows + slot * BLOCK, BLOCK)
        chosen = pick(0, slot)
        for part_at, held in ((0, kv), (1, vv)):
            columns = slice(part_at * kv_width, (part_at + 1) * kv_width)
            own = held[chosen]
            got = jnp.where(before, recv_kv[0, at, columns], own)
            got = jnp.where(after, recv_kv[1, at, columns], got)
            for g in range(KV_HEADS):
                win[g, home, part_at * D_HEAD:(part_at + 1) * D_HEAD] = got[
                    :, g * D_HEAD:(g + 1) * D_HEAD
                ]

    def win_copy(hop, g, place, rank):
        here = win.at[g, pl.ds((place + core) * rows, rows), :]
        dst = place - hop if hop in (2, 4) else place
        there = win.at[g, pl.ds((dst + core) * rows, rows), :]
        index = {2: 0, 4: 1}.get(hop, 2 + place // 2)
        return remote(here, there, win_send.at[index, g], win_recv.at[index, g], rank)

    for g in range(KV_HEADS):
        for hop in (2, 4):
            @pl.when(me + hop < n)
            def _():
                win_copy(hop, g, 4, me + hop).start()
        win_copy(0, g, 4, partner).start()

    start_q(1)
    for g in range(2, KV_HEADS):
        prepare_q(g)

    for g in range(KV_HEADS):
        for hop in (2, 4):
            @pl.when(me >= hop)
            def _():
                win_copy(hop, g, 4, me + hop).wait_recv()
                win_copy(0, g, 4 - hop, partner).start()

    span = (REACH + 1) * rows - (recv - 1) * BLOCK
    scale = D_HEAD ** -0.5 * LOG2E

    for g in range(KV_HEADS):
        for d, distance, rank, sends, receives in routes:
            @pl.when(receives)
            def _():
                q_copy(d, g, rank).wait_recv()
        if g + 2 < KV_HEADS:
            start_q(g + 2)
        for slot in range(recv):
            before, after = source(slot)
            at = pl.ds(slot * BLOCK, BLOCK)
            chosen = pick(0, slot)
            for h in range(PER_GROUP):
                columns = slice(h * D_HEAD, (h + 1) * D_HEAD)
                own = qv[chosen, :, g * width + h * D_HEAD:g * width + (h + 1) * D_HEAD]
                got = jnp.where(before, recv_q[0, g, at, columns], own)
                got = jnp.where(after, recv_q[1, g, at, columns], got)
                qp[h, at, :] = got
        win_copy(0, g, 4, partner).wait_recv()
        for hop in (2, 4):
            @pl.when(me >= hop)
            def _():
                win_copy(0, g, 4 - hop, partner).wait_recv()

        for slot in range(recv):
            start = pl.multiple_of(core * rows + slot * BLOCK, BLOCK)
            at = slice(slot * BLOCK, (slot + 1) * BLOCK)

            def heads(pair, carry):
                keys = win[g, pl.ds(start, span), :D_HEAD]
                values = win[g, pl.ds(start, span), D_HEAD:]
                query = qp[pl.ds(pair * 2, 2), at, :].reshape(2 * BLOCK, D_HEAD)
                logits = lax.dot_general(
                    query, keys, (((1,), (1,)), ((), ())), preferred_element_type=jnp.float32
                )
                mask = bias[at, slot * BLOCK:slot * BLOCK + span]
                logits = logits.reshape(2, BLOCK, span) * scale + mask[None]
                top = jnp.max(logits, axis=-1, keepdims=True)
                raised = jnp.exp2(logits - top)
                totals = jnp.sum(raised, axis=-1, keepdims=True)
                weights = raised.astype(jnp.bfloat16).reshape(2 * BLOCK, span)
                head_out = jnp.dot(weights, values, preferred_element_type=jnp.float32)
                head_out = (head_out.reshape(2, BLOCK, D_HEAD) / totals).astype(jnp.bfloat16)
                for i in range(2):
                    head = g * PER_GROUP + pair * 2 + i
                    column = pl.multiple_of(head * D_HEAD, D_HEAD)
                    out_ref[at, pl.ds(column, D_HEAD)] = head_out[i]
                    score[at, :] += head_out[i].astype(jnp.float32) * dir_ref[pl.ds(head, 1), :]
                return carry

            lax.fori_loop(0, PER_GROUP // 2, heads, 0)

    next_first = meta_all[pl.ds(me + REACH + 1, 1)][0, 0:1, 0:1]
    following = jnp.where(row_at == rows - 1, next_first, cols_ref[1])
    token_score = jnp.sum(score[...], axis=-1, keepdims=True)
    chosen = (ids == lane_at) & (ids != following)
    partial = jnp.sum(jnp.where(chosen, token_score, 0.0), axis=0, keepdims=True)
    part[...] = jnp.broadcast_to(partial, part.shape)
    part_all[pl.ds(me, 1)] = part[...][None]
    tell_all(part, part_all, 0, part_send, part_recv)

    for d, distance, rank, sends, receives in routes:
        @pl.when(sends)
        def _():
            remote(send_kv.at[d], recv_kv.at[d], kv_send.at[d], kv_recv.at[d], rank).wait_send()
            for g in range(KV_HEADS):
                q_copy(d, g, rank).wait_send()
    for g in range(KV_HEADS):
        win_copy(0, g, 4, partner).wait_send()
        for hop in (2, 4):
            @pl.when(me + hop < n)
            def _():
                win_copy(hop, g, 4, me + hop).wait_send()

            @pl.when(me >= hop)
            def _():
                win_copy(0, g, 4 - hop, partner).wait_send()

    hear_all(part, part_all, 0, part_send, part_recv)
    rew_ref[...] = jnp.sum(part_all[...], axis=0)


def shards(queries, keys, values, block_counts, segment_ids, reward_dir):
    n = lax.axis_size("dp")
    rows = segment_ids.shape[0]
    cap = queries.shape[0] // BLOCK
    kv_width = keys.shape[1]
    width = PER_GROUP * D_HEAD
    id_rows = rows // LANES
    meta = jnp.concatenate([
        segment_ids.reshape(id_rows, LANES),
        jnp.broadcast_to(block_counts[:, None], (8 - id_rows, LANES)),
    ])
    following = jnp.concatenate([segment_ids[1:], segment_ids[-1:]])
    cols = jnp.broadcast_to(jnp.stack([segment_ids, following])[:, :, None], (2, rows, LANES))
    vmem = pl.BlockSpec(memory_space=pltpu.VMEM)
    hbm = pl.BlockSpec(memory_space=pl.ANY)
    dma = pltpu.SemaphoreType.DMA
    bf16 = jnp.bfloat16
    attn_out, rewards = pl.pallas_call(
        functools.partial(kernel, n),
        out_shape=(
            jax.ShapeDtypeStruct((rows, HEADS * D_HEAD), bf16),
            jax.ShapeDtypeStruct((8, LANES), jnp.float32),
        ),
        in_specs=[hbm, hbm, hbm, vmem, vmem, vmem],
        out_specs=(vmem, vmem),
        scratch_shapes=[
            pltpu.VMEM((cap, BLOCK, HEADS * D_HEAD), bf16),
            pltpu.VMEM((cap, BLOCK, kv_width), bf16),
            pltpu.VMEM((cap, BLOCK, kv_width), bf16),
            pltpu.VMEM((n + REACH + 1, 8, LANES), jnp.int32),
            pltpu.VMEM((2, KV_HEADS, rows, width), bf16),
            pltpu.VMEM((2, KV_HEADS, rows, width), bf16),
            pltpu.VMEM((2, rows, 2 * kv_width), bf16),
            pltpu.VMEM((2, rows, 2 * kv_width), bf16),
            pltpu.VMEM((KV_HEADS, (REACH + 2) * rows, 2 * D_HEAD), bf16),
            pltpu.VMEM((PER_GROUP, rows, D_HEAD), bf16),
            pltpu.VMEM((rows, (REACH + 1) * rows), jnp.float32),
            pltpu.VMEM((rows, LANES), jnp.float32),
            pltpu.VMEM((8, LANES), jnp.float32),
            pltpu.VMEM((n, 8, LANES), jnp.float32),
            dma((3,)),
            dma((n,)), dma((n,)),
            dma((2,)), dma((2,)),
            dma((2, KV_HEADS)), dma((2, KV_HEADS)),
            dma((5, KV_HEADS)), dma((5, KV_HEADS)),
            dma((n,)), dma((n,)),
        ],
        compiler_params=pltpu.CompilerParams(
            collective_id=0, has_side_effects=True, vmem_limit_bytes=56 * 1024 * 1024
        ),
    )(
        queries.reshape(cap, BLOCK, -1), keys.reshape(cap, BLOCK, -1),
        values.reshape(cap, BLOCK, -1), meta, cols, reward_dir.reshape(HEADS, D_HEAD),
    )
    response_count = n * 2 // REACH
    return attn_out, rewards[0, :response_count]


def solution(mesh):
    return jax.shard_map(
        shards,
        mesh=mesh,
        in_specs=(
            P(("groups", "dp"), None),
            P(("groups", "dp"), None),
            P(("groups", "dp"), None),
            P(("groups", "dp")),
            P(("groups", "dp")),
            P(),
        ),
        out_specs=(P(("groups", "dp"), None), P("groups")),
        check_vma=False,
    )
```

```python
import functools

import jax
import jax.numpy as jnp
from jax import lax
from jax.experimental import pallas as pl
from jax.experimental.pallas import tpu as pltpu
from jax.sharding import PartitionSpec as P

D_HEAD = 128
HEADS = 32
KV_HEADS = 4
BLOCK = 128
REACH = 4
LANES = 128
PER_GROUP = HEADS // KV_HEADS
PER_CHUNK = 4
CHUNKS = HEADS // PER_CHUNK
AHEAD = 3
LOG2E = 1.4426950408889634
MASKED = -1e30


def kernel(
    n, q_hbm, k_hbm, v_hbm, count_ref, ids_ref, dir_ref, out_ref, rew_ref,
    meta_ref, qv, kv, vv, meta_all, send_q, recv_q, send_kv, recv_kv, win, qp, bias, score,
    part, part_all,
    load_sem, meta_send, meta_recv, kv_send, kv_recv, q_send, q_recv,
    win_send, win_recv, part_send, part_recv,
):
    me = lax.axis_index("dp")
    core = lax.rem(me, 2)
    partner = me + 1 - 2 * core
    rows = ids_ref.shape[1]
    recv = rows // BLOCK
    cap = qv.shape[0]
    width = PER_CHUNK * D_HEAD
    kv_width = KV_HEADS * D_HEAD
    id_rows = rows // LANES

    loads = [
        pltpu.make_async_copy(k_hbm, kv, load_sem.at[0]),
        pltpu.make_async_copy(v_hbm, vv, load_sem.at[1]),
        pltpu.make_async_copy(q_hbm, qv, load_sem.at[2]),
    ]
    for load in loads:
        load.start()

    count = count_ref[0]
    meta_ref[...] = jnp.full((8, LANES), count, jnp.int32)
    for i in range(id_rows):
        meta_ref[i:i + 1, :] = ids_ref[:, i * LANES:(i + 1) * LANES]
    for pad in list(range(REACH)) + [n + REACH]:
        meta_all[pad] = jnp.full((8, LANES), -1, jnp.int32)
    meta_all[pl.ds(me + REACH, 1)] = meta_ref[...][None]
    for distance in (2, 4):
        @pl.when(me < distance)
        def _():
            win[:, pl.ds((4 - distance) * rows, 2 * rows), :] = jnp.zeros(
                (KV_HEADS, 2 * rows, 2 * D_HEAD), win.dtype
            )
    score[...] = jnp.zeros_like(score)

    barrier = pltpu.get_barrier_semaphore()

    def greet(i, carry):
        pl.semaphore_signal(
            barrier, inc=1, device_id={"dp": lax.rem(me + i, n)},
            device_id_type=pl.DeviceIdType.MESH,
        )
        return carry

    lax.fori_loop(1, n, greet, 0)
    pl.semaphore_wait(barrier, n - 1)

    def remote(src, dst, send_sem, recv_sem, rank):
        return pltpu.make_async_remote_copy(
            src_ref=src, dst_ref=dst, send_sem=send_sem, recv_sem=recv_sem,
            device_id={"dp": rank}, device_id_type=pl.DeviceIdType.MESH,
        )

    def tell_all(src, table, shift, send_sem, recv_sem):
        def begin(i, carry):
            remote(src, table.at[me + shift], send_sem.at[i], recv_sem.at[i],
                   lax.rem(me + i, n)).start()
            return carry

        lax.fori_loop(1, n, begin, 0)

    def hear_all(src, table, shift, send_sem, recv_sem):
        def finish(i, carry):
            came = lax.rem(me + n - i, n)
            remote(src, table.at[came + shift], send_sem.at[i], recv_sem.at[i],
                   lax.rem(me + i, n)).wait()
            return carry

        lax.fori_loop(1, n, finish, 0)

    tell_all(meta_ref, meta_all, REACH, meta_send, meta_recv)
    hear_all(meta_ref, meta_all, REACH, meta_send, meta_recv)

    counts = meta_all[REACH:REACH + n, id_rows, :]
    rank_index = lax.broadcasted_iota(jnp.int32, (n, LANES), 0)
    offset = jnp.sum(jnp.where(rank_index < me, counts, 0), axis=0, keepdims=True)[0, 0]

    def pick(distance, slot):
        return jnp.clip((me + distance) * recv + slot - offset, 0, cap - 1)

    routes = ((0, 1, me + 1, me < n - 1, me > 0), (1, -1, me - 1, me > 0, me < n - 1))

    def both(start_or_wait):
        for d, distance, rank, sends, receives in routes:
            start_or_wait(d, rank, sends, receives)

    for load in loads[:2]:
        load.wait()
    for d, distance, rank, sends, receives in routes:
        for slot in range(recv):
            at = pl.ds(slot * BLOCK, BLOCK)
            chosen = pick(distance, slot)
            send_kv[d, at, :kv_width] = kv[chosen]
            send_kv[d, at, kv_width:] = vv[chosen]

        @pl.when(sends)
        def _():
            remote(send_kv.at[d], recv_kv.at[d], kv_send.at[d], kv_recv.at[d], rank).start()

    loads[2].wait()

    def prepare_q(g):
        for d, distance, rank, sends, receives in routes:
            for slot in range(recv):
                send_q[d, g, pl.ds(slot * BLOCK, BLOCK), :] = qv[
                    pick(distance, slot), :, g * width:(g + 1) * width
                ]

    def q_copy(d, g, rank):
        return remote(send_q.at[d, g], recv_q.at[d, g], q_send.at[d, g], q_recv.at[d, g], rank)

    def start_q(g):
        for d, distance, rank, sends, receives in routes:
            @pl.when(sends)
            def _():
                q_copy(d, g, rank).start()

    prepare_q(0)
    start_q(0)
    for c in range(1, CHUNKS):
        prepare_q(c)

    row_at = lax.broadcasted_iota(jnp.int32, (rows, LANES), 0)
    lane_at = lax.broadcasted_iota(jnp.int32, (rows, LANES), 1)
    ids = jnp.concatenate([
        jnp.transpose(jnp.broadcast_to(ids_ref[:, i * LANES:(i + 1) * LANES], (LANES, LANES)))
        for i in range(id_rows)
    ])
    for chunk in range((REACH + 1) * id_rows):
        key_ids = meta_all[pl.ds(me + chunk // id_rows, 1)][0, chunk % id_rows:chunk % id_rows + 1, :]
        key_at = lane_at + (chunk * LANES - REACH * rows)
        bias[:, chunk * LANES:(chunk + 1) * LANES] = jnp.where(
            (ids == key_ids) & (key_at <= row_at), 0.0, MASKED
        )

    for d, distance, rank, sends, receives in routes:
        @pl.when(receives)
        def _():
            remote(send_kv.at[d], recv_kv.at[d], kv_send.at[d], kv_recv.at[d], rank).wait_recv()

    def source(slot):
        block = me * recv + slot
        return block < offset, block >= offset + count

    for slot in range(recv):
        before, after = source(slot)
        at = pl.ds(slot * BLOCK, BLOCK)
        home = pl.ds((4 + core) * rows + slot * BLOCK, BLOCK)
        chosen = pick(0, slot)
        for part_at, held in ((0, kv), (1, vv)):
            columns = slice(part_at * kv_width, (part_at + 1) * kv_width)
            own = held[chosen]
            got = jnp.where(before, recv_kv[0, at, columns], own)
            got = jnp.where(after, recv_kv[1, at, columns], got)
            for g in range(KV_HEADS):
                win[g, home, part_at * D_HEAD:(part_at + 1) * D_HEAD] = got[
                    :, g * D_HEAD:(g + 1) * D_HEAD
                ]

    def win_copy(hop, g, place, rank):
        here = win.at[g, pl.ds((place + core) * rows, rows), :]
        dst = place - hop if hop in (2, 4) else place
        there = win.at[g, pl.ds((dst + core) * rows, rows), :]
        index = {2: 0, 4: 1}.get(hop, 2 + place // 2)
        return remote(here, there, win_send.at[index, g], win_recv.at[index, g], rank)

    def start_win(g):
        for hop in (2, 4):
            @pl.when(me + hop < n)
            def _():
                win_copy(hop, g, 4, me + hop).start()
        win_copy(0, g, 4, partner).start()

    def forward_win(g):
        for hop in (2, 4):
            @pl.when(me >= hop)
            def _():
                win_copy(hop, g, 4, me + hop).wait_recv()
                win_copy(0, g, 4 - hop, partner).start()

    start_win(0)
    start_q(1)
    start_win(1)
    start_q(2)
    forward_win(0)

    span = (REACH + 1) * rows - (recv - 1) * BLOCK
    scale = D_HEAD ** -0.5 * LOG2E

    for c in range(CHUNKS):
        g = c * PER_CHUNK // PER_GROUP
        opens = c * PER_CHUNK % PER_GROUP == 0
        for d, distance, rank, sends, receives in routes:
            @pl.when(receives)
            def _():
                q_copy(d, c, rank).wait_recv()
        if c + AHEAD < CHUNKS:
            start_q(c + AHEAD)
        for slot in range(recv):
            before, after = source(slot)
            at = pl.ds(slot * BLOCK, BLOCK)
            chosen = pick(0, slot)
            for h in range(PER_CHUNK):
                columns = slice(h * D_HEAD, (h + 1) * D_HEAD)
                own = qv[chosen, :, c * width + h * D_HEAD:c * width + (h + 1) * D_HEAD]
                got = jnp.where(before, recv_q[0, c, at, columns], own)
                got = jnp.where(after, recv_q[1, c, at, columns], got)
                qp[h, at, :] = got
        if opens:
            win_copy(0, g, 4, partner).wait_recv()
            for hop in (2, 4):
                @pl.when(me >= hop)
                def _():
                    win_copy(0, g, 4 - hop, partner).wait_recv()

        for slot in range(recv):
            start = pl.multiple_of(core * rows + slot * BLOCK, BLOCK)
            at = slice(slot * BLOCK, (slot + 1) * BLOCK)
            keys = win.at[g, pl.ds(start, span), :D_HEAD]
            values = win.at[g, pl.ds(start, span), D_HEAD:]
            for pair in range(PER_CHUNK // 2):
                query = qp[pair * 2:pair * 2 + 2, at, :].reshape(2 * BLOCK, D_HEAD)
                logits = lax.dot_general(
                    query, keys[...], (((1,), (1,)), ((), ())),
                    preferred_element_type=jnp.float32,
                )
                mask = bias[at, slot * BLOCK:slot * BLOCK + span]
                logits = logits.reshape(2, BLOCK, span) * scale + mask[None]
                top = jnp.max(logits, axis=-1, keepdims=True)
                raised = jnp.exp2(logits - top)
                totals = jnp.sum(raised, axis=-1, keepdims=True)
                weights = raised.astype(jnp.bfloat16).reshape(2 * BLOCK, span)
                head_out = jnp.dot(weights, values[...], preferred_element_type=jnp.float32)
                head_out = (head_out.reshape(2, BLOCK, D_HEAD) / totals).astype(jnp.bfloat16)
                for i in range(2):
                    head = c * PER_CHUNK + pair * 2 + i
                    out_ref[at, head * D_HEAD:(head + 1) * D_HEAD] = head_out[i]
                    score[at, :] += head_out[i].astype(jnp.float32) * dir_ref[head:head + 1, :]

        if opens and g + 1 < KV_HEADS:
            forward_win(g + 1)
            if g + 2 < KV_HEADS:
                start_win(g + 2)

    next_first = meta_all[pl.ds(me + REACH + 1, 1)][0, 0:1, 0:1]
    following = jnp.where(row_at == rows - 1, next_first, pltpu.roll(ids, rows - 1, 0))
    token_score = jnp.sum(score[...], axis=-1, keepdims=True)
    chosen = (ids == lane_at) & (ids != following)
    partial = jnp.sum(jnp.where(chosen, token_score, 0.0), axis=0, keepdims=True)
    part[...] = jnp.broadcast_to(partial, part.shape)
    part_all[pl.ds(me, 1)] = part[...][None]
    tell_all(part, part_all, 0, part_send, part_recv)

    for d, distance, rank, sends, receives in routes:
        @pl.when(sends)
        def _():
            remote(send_kv.at[d], recv_kv.at[d], kv_send.at[d], kv_recv.at[d], rank).wait_send()
            for c in range(CHUNKS):
                q_copy(d, c, rank).wait_send()
    for g in range(KV_HEADS):
        win_copy(0, g, 4, partner).wait_send()
        for hop in (2, 4):
            @pl.when(me + hop < n)
            def _():
                win_copy(hop, g, 4, me + hop).wait_send()

            @pl.when(me >= hop)
            def _():
                win_copy(0, g, 4 - hop, partner).wait_send()

    hear_all(part, part_all, 0, part_send, part_recv)
    rew_ref[...] = jnp.sum(part_all[...], axis=0)[0:1, :rew_ref.shape[1]]


def shards(queries, keys, values, block_counts, segment_ids, reward_dir):
    n = lax.axis_size("dp")
    rows = segment_ids.shape[0]
    cap = queries.shape[0] // BLOCK
    kv_width = keys.shape[1]
    width = PER_CHUNK * D_HEAD
    response_count = n * 2 // REACH
    vmem = pl.BlockSpec(memory_space=pltpu.VMEM)
    hbm = pl.BlockSpec(memory_space=pl.ANY)
    dma = pltpu.SemaphoreType.DMA
    bf16 = jnp.bfloat16
    attn_out, rewards = pl.pallas_call(
        functools.partial(kernel, n),
        out_shape=(
            jax.ShapeDtypeStruct((rows, HEADS * D_HEAD), bf16),
            jax.ShapeDtypeStruct((1, response_count), jnp.float32),
        ),
        in_specs=[hbm, hbm, hbm, pl.BlockSpec(memory_space=pltpu.SMEM), vmem, vmem],
        out_specs=(vmem, vmem),
        scratch_shapes=[
            pltpu.VMEM((8, LANES), jnp.int32),
            pltpu.VMEM((cap, BLOCK, HEADS * D_HEAD), bf16),
            pltpu.VMEM((cap, BLOCK, kv_width), bf16),
            pltpu.VMEM((cap, BLOCK, kv_width), bf16),
            pltpu.VMEM((n + REACH + 1, 8, LANES), jnp.int32),
            pltpu.VMEM((2, CHUNKS, rows, width), bf16),
            pltpu.VMEM((2, CHUNKS, rows, width), bf16),
            pltpu.VMEM((2, rows, 2 * kv_width), bf16),
            pltpu.VMEM((2, rows, 2 * kv_width), bf16),
            pltpu.VMEM((KV_HEADS, (REACH + 2) * rows, 2 * D_HEAD), bf16),
            pltpu.VMEM((PER_CHUNK, rows, D_HEAD), bf16),
            pltpu.VMEM((rows, (REACH + 1) * rows), jnp.float32),
            pltpu.VMEM((rows, LANES), jnp.float32),
            pltpu.VMEM((8, LANES), jnp.float32),
            pltpu.VMEM((n, 8, LANES), jnp.float32),
            dma((3,)),
            dma((n,)), dma((n,)),
            dma((2,)), dma((2,)),
            dma((2, CHUNKS)), dma((2, CHUNKS)),
            dma((5, KV_HEADS)), dma((5, KV_HEADS)),
            dma((n,)), dma((n,)),
        ],
        compiler_params=pltpu.CompilerParams(
            collective_id=0, has_side_effects=True, vmem_limit_bytes=56 * 1024 * 1024
        ),
    )(
        queries.reshape(cap, BLOCK, -1), keys.reshape(cap, BLOCK, -1),
        values.reshape(cap, BLOCK, -1), block_counts, segment_ids.reshape(1, rows), reward_dir.reshape(HEADS, D_HEAD),
    )
    return attn_out, rewards.reshape(response_count)


def solution(mesh):
    return jax.shard_map(
        shards,
        mesh=mesh,
        in_specs=(
            P(("groups", "dp"), None),
            P(("groups", "dp"), None),
            P(("groups", "dp"), None),
            P(("groups", "dp")),
            P(("groups", "dp")),
            P(),
        ),
        out_specs=(P(("groups", "dp"), None), P("groups")),
        check_vma=False,
    )
```

```python
import functools

import jax
import jax.numpy as jnp
from jax import lax
from jax.experimental import pallas as pl
from jax.experimental.pallas import tpu as pltpu
from jax.sharding import PartitionSpec as P

D_HEAD = 128
HEADS = 32
KV_HEADS = 4
BLOCK = 128
REACH = 4
LANES = 128
PER_GROUP = HEADS // KV_HEADS
PER_CHUNK = 4
CHUNKS = HEADS // PER_CHUNK
AHEAD = 4
PLANE = 4
LOG2E = 1.4426950408889634
MASKED = -1e30


def kernel(
    n, q_hbm, k_hbm, v_hbm, count_ref, ids_ref, dir_ref, out_ref, rew_ref,
    meta_ref, qv, kv, vv, meta_all, send_q, recv_q, send_kv, recv_kv, win, qp, bias, score,
    part, part_all, relay, out_buf,
    load_sem, meta_send, meta_recv, kv_send, kv_recv, q_send, q_recv,
    win_send, win_recv, part_send, part_recv, relay_send, relay_recv, out_sem,
):
    me = lax.axis_index("dp")
    core = lax.rem(me, 2)
    partner = me + 1 - 2 * core
    rows = ids_ref.shape[1]
    recv = rows // BLOCK
    cap = qv.shape[0]
    width = PER_CHUNK * D_HEAD
    kv_width = KV_HEADS * D_HEAD
    id_rows = rows // LANES

    loads = [
        pltpu.make_async_copy(k_hbm, kv, load_sem.at[0]),
        pltpu.make_async_copy(v_hbm, vv, load_sem.at[1]),
        pltpu.make_async_copy(q_hbm, qv, load_sem.at[2]),
    ]
    for load in loads:
        load.start()

    count = count_ref[0]
    meta_ref[...] = jnp.full((8, LANES), count, jnp.int32)
    for i in range(id_rows):
        meta_ref[i:i + 1, :] = ids_ref[:, i * LANES:(i + 1) * LANES]
    for pad in list(range(REACH)) + [n + REACH]:
        meta_all[pad] = jnp.full((8, LANES), -1, jnp.int32)
    meta_all[pl.ds(me + REACH, 1)] = meta_ref[...][None]
    for distance in (2, 4):
        @pl.when(me < distance)
        def _():
            win[:, pl.ds((4 - distance) * rows, 2 * rows), :] = jnp.zeros(
                (KV_HEADS, 2 * rows, 2 * D_HEAD), win.dtype
            )
    score[...] = jnp.zeros_like(score)

    barrier = pltpu.get_barrier_semaphore()

    def greet(i, carry):
        pl.semaphore_signal(
            barrier, inc=1, device_id={"dp": lax.rem(me + i, n)},
            device_id_type=pl.DeviceIdType.MESH,
        )
        return carry

    lax.fori_loop(1, n, greet, 0)
    pl.semaphore_wait(barrier, n - 1)

    def remote(src, dst, send_sem, recv_sem, rank):
        return pltpu.make_async_remote_copy(
            src_ref=src, dst_ref=dst, send_sem=send_sem, recv_sem=recv_sem,
            device_id={"dp": rank}, device_id_type=pl.DeviceIdType.MESH,
        )

    def tell_all(src, table, shift, send_sem, recv_sem):
        def begin(i, carry):
            remote(src, table.at[me + shift], send_sem.at[i], recv_sem.at[i],
                   lax.rem(me + i, n)).start()
            return carry

        lax.fori_loop(1, n, begin, 0)

    def hear_all(src, table, shift, send_sem, recv_sem):
        def finish(i, carry):
            came = lax.rem(me + n - i, n)
            remote(src, table.at[came + shift], send_sem.at[i], recv_sem.at[i],
                   lax.rem(me + i, n)).wait()
            return carry

        lax.fori_loop(1, n, finish, 0)

    tell_all(meta_ref, meta_all, REACH, meta_send, meta_recv)
    hear_all(meta_ref, meta_all, REACH, meta_send, meta_recv)

    counts = meta_all[REACH:REACH + n, id_rows, :]
    rank_index = lax.broadcasted_iota(jnp.int32, (n, LANES), 0)
    offset = jnp.sum(jnp.where(rank_index < me, counts, 0), axis=0, keepdims=True)[0, 0]

    def pick(distance, slot):
        return jnp.clip((me + distance) * recv + slot - offset, 0, cap - 1)

    routes = ((0, 1, me + 1, me < n - 1, me > 0), (1, -1, me - 1, me > 0, me < n - 1))

    def both(start_or_wait):
        for d, distance, rank, sends, receives in routes:
            start_or_wait(d, rank, sends, receives)

    for load in loads[:2]:
        load.wait()
    for d, distance, rank, sends, receives in routes:
        for slot in range(recv):
            at = pl.ds(slot * BLOCK, BLOCK)
            chosen = pick(distance, slot)
            send_kv[d, at, :kv_width] = kv[chosen]
            send_kv[d, at, kv_width:] = vv[chosen]

        @pl.when(sends)
        def _():
            remote(send_kv.at[d], recv_kv.at[d], kv_send.at[d], kv_recv.at[d], rank).start()

    loads[2].wait()

    def prepare_q(g):
        for d, distance, rank, sends, receives in routes:
            for slot in range(recv):
                send_q[d, g, pl.ds(slot * BLOCK, BLOCK), :] = qv[
                    pick(distance, slot), :, g * width:(g + 1) * width
                ]

    def q_copy(d, g, rank):
        return remote(send_q.at[d, g], recv_q.at[d, g], q_send.at[d, g], q_recv.at[d, g], rank)

    place = lax.rem(me, PLANE)
    plane = me // PLANE
    planes = n // PLANE

    def early(border, c):
        return (c * 3 % CHUNKS) * planes < (planes - 1 - border) * CHUNKS

    def crosses(d):
        return place == (PLANE - 1 if d == 0 else 0)

    def relay_out(d, c):
        border = plane if d == 0 else plane - 1
        near, far = (-2, 4) if d == 0 else (-4, 2)
        rank = jnp.where(early(border, c), me + near, me + far)
        return remote(send_q.at[d, c], relay.at[c], q_send.at[d, c], relay_recv.at[c], rank)

    relay_d = 1 - lax.rem(place, 2)
    relay_to = jnp.where(place < 2, me + 3, me - 3)
    relay_border = jnp.where(place < 2, plane, plane - 1)
    relay_open = (relay_border >= 0) & (relay_border < planes - 1)

    def relays(c):
        return relay_open & (early(relay_border, c) == (place < 2))

    def relay_on(c):
        return remote(
            relay.at[c], recv_q.at[relay_d, c], relay_send.at[c], q_recv.at[relay_d, c], relay_to
        )

    def forward_q(c):
        @pl.when(relays(c))
        def _():
            remote(relay.at[c], relay.at[c], relay_send.at[c], relay_recv.at[c], relay_to).wait_recv()
            relay_on(c).start()

    def start_q(g):
        for d, distance, rank, sends, receives in routes:
            @pl.when(sends & crosses(d))
            def _():
                relay_out(d, g).start()

            @pl.when(sends & jnp.logical_not(crosses(d)))
            def _():
                q_copy(d, g, rank).start()

    prepare_q(0)
    start_q(0)
    for c in range(1, CHUNKS):
        prepare_q(c)

    row_at = lax.broadcasted_iota(jnp.int32, (rows, LANES), 0)
    lane_at = lax.broadcasted_iota(jnp.int32, (rows, LANES), 1)
    ids = jnp.concatenate([
        jnp.transpose(jnp.broadcast_to(ids_ref[:, i * LANES:(i + 1) * LANES], (LANES, LANES)))
        for i in range(id_rows)
    ])
    for chunk in range((REACH + 1) * id_rows):
        key_ids = meta_all[pl.ds(me + chunk // id_rows, 1)][0, chunk % id_rows:chunk % id_rows + 1, :]
        key_at = lane_at + (chunk * LANES - REACH * rows)
        bias[:, chunk * LANES:(chunk + 1) * LANES] = jnp.where(
            (ids == key_ids) & (key_at <= row_at), 0.0, MASKED
        )

    for d, distance, rank, sends, receives in routes:
        @pl.when(receives)
        def _():
            remote(send_kv.at[d], recv_kv.at[d], kv_send.at[d], kv_recv.at[d], rank).wait_recv()

    def source(slot):
        block = me * recv + slot
        return block < offset, block >= offset + count

    for slot in range(recv):
        before, after = source(slot)
        at = pl.ds(slot * BLOCK, BLOCK)
        home = pl.ds((4 + core) * rows + slot * BLOCK, BLOCK)
        chosen = pick(0, slot)
        for part_at, held in ((0, kv), (1, vv)):
            columns = slice(part_at * kv_width, (part_at + 1) * kv_width)
            own = held[chosen]
            got = jnp.where(before, recv_kv[0, at, columns], own)
            got = jnp.where(after, recv_kv[1, at, columns], got)
            for g in range(KV_HEADS):
                win[g, home, part_at * D_HEAD:(part_at + 1) * D_HEAD] = got[
                    :, g * D_HEAD:(g + 1) * D_HEAD
                ]

    def win_copy(hop, g, place, rank):
        here = win.at[g, pl.ds((place + core) * rows, rows), :]
        dst = place - hop if hop in (2, 4) else place
        there = win.at[g, pl.ds((dst + core) * rows, rows), :]
        index = {2: 0, 4: 1}.get(hop, 2 + place // 2)
        return remote(here, there, win_send.at[index, g], win_recv.at[index, g], rank)

    def start_win(g):
        for hop in (2, 4):
            @pl.when(me + hop < n)
            def _():
                win_copy(hop, g, 4, me + hop).start()
        win_copy(0, g, 4, partner).start()

    def forward_win(g):
        for hop in (2, 4):
            @pl.when(me >= hop)
            def _():
                win_copy(hop, g, 4, me + hop).wait_recv()
                win_copy(0, g, 4 - hop, partner).start()

    start_win(0)
    start_q(1)
    forward_q(0)
    start_win(1)
    start_q(2)
    forward_win(0)
    start_q(3)
    forward_q(1)

    span = (REACH + 1) * rows - (recv - 1) * BLOCK
    scale = D_HEAD ** -0.5 * LOG2E

    def out_copy(c):
        columns = pl.ds(c * width, width)
        return pltpu.make_async_copy(out_buf.at[:, columns], out_ref.at[:, columns], out_sem.at[c])

    for c in range(CHUNKS):
        g = c * PER_CHUNK // PER_GROUP
        opens = c * PER_CHUNK % PER_GROUP == 0
        for d, distance, rank, sends, receives in routes:
            @pl.when(receives)
            def _():
                q_copy(d, c, rank).wait_recv()
        if c + AHEAD < CHUNKS:
            start_q(c + AHEAD)
        for slot in range(recv):
            before, after = source(slot)
            at = pl.ds(slot * BLOCK, BLOCK)
            chosen = pick(0, slot)
            for h in range(PER_CHUNK):
                columns = slice(h * D_HEAD, (h + 1) * D_HEAD)
                own = qv[chosen, :, c * width + h * D_HEAD:c * width + (h + 1) * D_HEAD]
                got = jnp.where(before, recv_q[0, c, at, columns], own)
                got = jnp.where(after, recv_q[1, c, at, columns], got)
                qp[h, at, :] = got
        if opens:
            win_copy(0, g, 4, partner).wait_recv()
            for hop in (2, 4):
                @pl.when(me >= hop)
                def _():
                    win_copy(0, g, 4 - hop, partner).wait_recv()

        for slot in range(recv):
            if slot == 1 and c + 2 < CHUNKS:
                forward_q(c + 2)
            start = pl.multiple_of(core * rows + slot * BLOCK, BLOCK)
            at = slice(slot * BLOCK, (slot + 1) * BLOCK)
            keys = win.at[g, pl.ds(start, span), :D_HEAD]
            values = win.at[g, pl.ds(start, span), D_HEAD:]
            for pair in range(PER_CHUNK // 2):
                query = qp[pair * 2:pair * 2 + 2, at, :].reshape(2 * BLOCK, D_HEAD)
                logits = lax.dot_general(
                    query, keys[...], (((1,), (1,)), ((), ())),
                    preferred_element_type=jnp.float32,
                )
                mask = bias[at, slot * BLOCK:slot * BLOCK + span]
                logits = logits.reshape(2, BLOCK, span) * scale + mask[None]
                top = jnp.max(logits, axis=-1, keepdims=True)
                raised = jnp.exp2(logits - top)
                totals = jnp.sum(raised, axis=-1, keepdims=True)
                weights = raised.astype(jnp.bfloat16).reshape(2 * BLOCK, span)
                head_out = jnp.dot(weights, values[...], preferred_element_type=jnp.float32)
                head_out = (head_out.reshape(2, BLOCK, D_HEAD) / totals).astype(jnp.bfloat16)
                for i in range(2):
                    head = c * PER_CHUNK + pair * 2 + i
                    out_buf[at, head * D_HEAD:(head + 1) * D_HEAD] = head_out[i]
                    score[at, :] += head_out[i].astype(jnp.float32) * dir_ref[head:head + 1, :]

        out_copy(c).start()
        if opens and g + 1 < KV_HEADS:
            forward_win(g + 1)
            if g + 2 < KV_HEADS:
                start_win(g + 2)

    next_first = meta_all[pl.ds(me + REACH + 1, 1)][0, 0:1, 0:1]
    following = jnp.where(row_at == rows - 1, next_first, pltpu.roll(ids, rows - 1, 0))
    token_score = jnp.sum(score[...], axis=-1, keepdims=True)
    chosen = (ids == lane_at) & (ids != following)
    partial = jnp.sum(jnp.where(chosen, token_score, 0.0), axis=0, keepdims=True)
    part[...] = jnp.broadcast_to(partial, part.shape)
    part_all[pl.ds(me, 1)] = part[...][None]
    tell_all(part, part_all, 0, part_send, part_recv)

    for d, distance, rank, sends, receives in routes:
        @pl.when(sends)
        def _():
            remote(send_kv.at[d], recv_kv.at[d], kv_send.at[d], kv_recv.at[d], rank).wait_send()
            for c in range(CHUNKS):
                q_copy(d, c, rank).wait_send()
    for g in range(KV_HEADS):
        win_copy(0, g, 4, partner).wait_send()
        for hop in (2, 4):
            @pl.when(me + hop < n)
            def _():
                win_copy(hop, g, 4, me + hop).wait_send()

            @pl.when(me >= hop)
            def _():
                win_copy(0, g, 4 - hop, partner).wait_send()

    for c in range(CHUNKS):
        @pl.when(relays(c))
        def _():
            relay_on(c).wait_send()

        out_copy(c).wait()
    hear_all(part, part_all, 0, part_send, part_recv)
    rew_ref[...] = jnp.sum(part_all[...], axis=0)[0:1, :rew_ref.shape[1]]


def shards(queries, keys, values, block_counts, segment_ids, reward_dir):
    n = lax.axis_size("dp")
    rows = segment_ids.shape[0]
    cap = queries.shape[0] // BLOCK
    kv_width = keys.shape[1]
    width = PER_CHUNK * D_HEAD
    response_count = n * 2 // REACH
    vmem = pl.BlockSpec(memory_space=pltpu.VMEM)
    hbm = pl.BlockSpec(memory_space=pl.ANY)
    dma = pltpu.SemaphoreType.DMA
    bf16 = jnp.bfloat16
    attn_out, rewards = pl.pallas_call(
        functools.partial(kernel, n),
        out_shape=(
            jax.ShapeDtypeStruct((rows, HEADS * D_HEAD), bf16),
            jax.ShapeDtypeStruct((1, response_count), jnp.float32),
        ),
        in_specs=[hbm, hbm, hbm, pl.BlockSpec(memory_space=pltpu.SMEM), vmem, vmem],
        out_specs=(hbm, vmem),
        scratch_shapes=[
            pltpu.VMEM((8, LANES), jnp.int32),
            pltpu.VMEM((cap, BLOCK, HEADS * D_HEAD), bf16),
            pltpu.VMEM((cap, BLOCK, kv_width), bf16),
            pltpu.VMEM((cap, BLOCK, kv_width), bf16),
            pltpu.VMEM((n + REACH + 1, 8, LANES), jnp.int32),
            pltpu.VMEM((2, CHUNKS, rows, width), bf16),
            pltpu.VMEM((2, CHUNKS, rows, width), bf16),
            pltpu.VMEM((2, rows, 2 * kv_width), bf16),
            pltpu.VMEM((2, rows, 2 * kv_width), bf16),
            pltpu.VMEM((KV_HEADS, (REACH + 2) * rows, 2 * D_HEAD), bf16),
            pltpu.VMEM((PER_CHUNK, rows, D_HEAD), bf16),
            pltpu.VMEM((rows, (REACH + 1) * rows), jnp.float32),
            pltpu.VMEM((rows, LANES), jnp.float32),
            pltpu.VMEM((8, LANES), jnp.float32),
            pltpu.VMEM((n, 8, LANES), jnp.float32),
            pltpu.VMEM((CHUNKS, rows, width), bf16),
            pltpu.VMEM((rows, HEADS * D_HEAD), bf16),
            dma((3,)),
            dma((n,)), dma((n,)),
            dma((2,)), dma((2,)),
            dma((2, CHUNKS)), dma((2, CHUNKS)),
            dma((5, KV_HEADS)), dma((5, KV_HEADS)),
            dma((n,)), dma((n,)),
            dma((CHUNKS,)), dma((CHUNKS,)), dma((CHUNKS,)),
        ],
        compiler_params=pltpu.CompilerParams(
            collective_id=0, has_side_effects=True, vmem_limit_bytes=56 * 1024 * 1024
        ),
    )(
        queries.reshape(cap, BLOCK, -1), keys.reshape(cap, BLOCK, -1),
        values.reshape(cap, BLOCK, -1), block_counts, segment_ids.reshape(1, rows), reward_dir.reshape(HEADS, D_HEAD),
    )
    return attn_out, rewards.reshape(response_count)


def solution(mesh):
    return jax.shard_map(
        shards,
        mesh=mesh,
        in_specs=(
            P(("groups", "dp"), None),
            P(("groups", "dp"), None),
            P(("groups", "dp"), None),
            P(("groups", "dp")),
            P(("groups", "dp")),
            P(),
        ),
        out_specs=(P(("groups", "dp"), None), P("groups")),
        check_vma=False,
    )
```

```python
import functools

import jax
import jax.numpy as jnp
from jax import lax
from jax.experimental import pallas as pl
from jax.experimental.pallas import tpu as pltpu
from jax.sharding import PartitionSpec as P

D_HEAD = 128
HEADS = 32
KV_HEADS = 4
BLOCK = 128
REACH = 4
LANES = 128
PER_GROUP = HEADS // KV_HEADS
PER_CHUNK = 2
CHUNKS = HEADS // PER_CHUNK
AHEAD = 8
LEAD = 4
PARTS = 8
PLANE = 4
LOG2E = 1.4426950408889634
MASKED = -1e30


def kernel(
    n, q_hbm, k_hbm, v_hbm, count_ref, ids_ref, dir_ref, out_ref, rew_ref,
    meta_ref, qv, kv, vv, meta_all, send_q, recv_q, send_kv, recv_kv, win, qp, bias, score,
    part, part_all, relay, out_buf,
    load_sem, meta_send, meta_recv, kv_send, kv_recv, q_send, q_recv,
    win_send, win_recv, part_send, part_recv, relay_send, relay_recv, out_sem,
):
    me = lax.axis_index("dp")
    core = lax.rem(me, 2)
    partner = me + 1 - 2 * core
    rows = ids_ref.shape[1]
    recv = rows // BLOCK
    cap = qv.shape[0]
    width = PER_CHUNK * D_HEAD
    kv_width = KV_HEADS * D_HEAD
    id_rows = rows // LANES

    loads = [
        pltpu.make_async_copy(k_hbm, kv, load_sem.at[0]),
        pltpu.make_async_copy(v_hbm, vv, load_sem.at[1]),
        pltpu.make_async_copy(q_hbm, qv, load_sem.at[2]),
    ]
    for load in loads:
        load.start()

    count = count_ref[0]
    meta_ref[...] = jnp.full((8, LANES), count, jnp.int32)
    for i in range(id_rows):
        meta_ref[i:i + 1, :] = ids_ref[:, i * LANES:(i + 1) * LANES]
    for pad in list(range(REACH)) + [n + REACH]:
        meta_all[pad] = jnp.full((8, LANES), -1, jnp.int32)
    meta_all[pl.ds(me + REACH, 1)] = meta_ref[...][None]
    for distance in (2, 4):
        @pl.when(me < distance)
        def _():
            win[:, pl.ds((4 - distance) * rows, 2 * rows), :] = jnp.zeros(
                (KV_HEADS, 2 * rows, 2 * D_HEAD), win.dtype
            )
    score[...] = jnp.zeros_like(score)

    barrier = pltpu.get_barrier_semaphore()

    def greet(i, carry):
        pl.semaphore_signal(
            barrier, inc=1, device_id={"dp": lax.rem(me + i, n)},
            device_id_type=pl.DeviceIdType.MESH,
        )
        return carry

    lax.fori_loop(1, n, greet, 0)
    pl.semaphore_wait(barrier, n - 1)

    def remote(src, dst, send_sem, recv_sem, rank):
        return pltpu.make_async_remote_copy(
            src_ref=src, dst_ref=dst, send_sem=send_sem, recv_sem=recv_sem,
            device_id={"dp": rank}, device_id_type=pl.DeviceIdType.MESH,
        )

    def tell_all(src, table, shift, send_sem, recv_sem):
        def begin(i, carry):
            remote(src, table.at[me + shift], send_sem.at[i], recv_sem.at[i],
                   lax.rem(me + i, n)).start()
            return carry

        lax.fori_loop(1, n, begin, 0)

    def hear_all(src, table, shift, send_sem, recv_sem):
        def finish(i, carry):
            came = lax.rem(me + n - i, n)
            remote(src, table.at[came + shift], send_sem.at[i], recv_sem.at[i],
                   lax.rem(me + i, n)).wait()
            return carry

        lax.fori_loop(1, n, finish, 0)

    tell_all(meta_ref, meta_all, REACH, meta_send, meta_recv)
    hear_all(meta_ref, meta_all, REACH, meta_send, meta_recv)

    counts = meta_all[REACH:REACH + n, id_rows, :]
    rank_index = lax.broadcasted_iota(jnp.int32, (n, LANES), 0)
    offset = jnp.sum(jnp.where(rank_index < me, counts, 0), axis=0, keepdims=True)[0, 0]

    def pick(distance, slot):
        return jnp.clip((me + distance) * recv + slot - offset, 0, cap - 1)

    routes = ((0, 1, me + 1, me < n - 1, me > 0), (1, -1, me - 1, me > 0, me < n - 1))

    def both(start_or_wait):
        for d, distance, rank, sends, receives in routes:
            start_or_wait(d, rank, sends, receives)

    for load in loads[:2]:
        load.wait()
    for d, distance, rank, sends, receives in routes:
        for slot in range(recv):
            at = pl.ds(slot * BLOCK, BLOCK)
            chosen = pick(distance, slot)
            send_kv[d, at, :kv_width] = kv[chosen]
            send_kv[d, at, kv_width:] = vv[chosen]

        @pl.when(sends)
        def _():
            remote(send_kv.at[d], recv_kv.at[d], kv_send.at[d], kv_recv.at[d], rank).start()

    loads[2].wait()

    def prepare_q(g):
        for d, distance, rank, sends, receives in routes:
            for slot in range(recv):
                send_q[d, g, pl.ds(slot * BLOCK, BLOCK), :] = qv[
                    pick(distance, slot), :, g * width:(g + 1) * width
                ]

    def q_copy(d, g, rank):
        return remote(send_q.at[d, g], recv_q.at[d, g], q_send.at[d, g], q_recv.at[d, g], rank)

    place = lax.rem(me, PLANE)
    plane = me // PLANE
    planes = n // PLANE

    def early(border, c):
        return (c * 3 % CHUNKS) * planes < (planes - 1 - border) * CHUNKS

    def crosses(d):
        return place == (PLANE - 1 if d == 0 else 0)

    def relay_out(d, c):
        border = plane if d == 0 else plane - 1
        near, far = (-2, 4) if d == 0 else (-4, 2)
        rank = jnp.where(early(border, c), me + near, me + far)
        return remote(send_q.at[d, c], relay.at[c], q_send.at[d, c], relay_recv.at[c], rank)

    relay_d = 1 - lax.rem(place, 2)
    relay_to = jnp.where(place < 2, me + 3, me - 3)
    relay_border = jnp.where(place < 2, plane, plane - 1)
    relay_open = (relay_border >= 0) & (relay_border < planes - 1)

    def relays(c):
        return relay_open & (early(relay_border, c) == (place < 2))

    def relay_on(c):
        return remote(
            relay.at[c], recv_q.at[relay_d, c], relay_send.at[c], q_recv.at[relay_d, c], relay_to
        )

    def forward_q(c):
        @pl.when(relays(c))
        def _():
            remote(relay.at[c], relay.at[c], relay_send.at[c], relay_recv.at[c], relay_to).wait_recv()
            relay_on(c).start()

    def start_q(g):
        for d, distance, rank, sends, receives in routes:
            @pl.when(sends & crosses(d))
            def _():
                relay_out(d, g).start()

            @pl.when(sends & jnp.logical_not(crosses(d)))
            def _():
                q_copy(d, g, rank).start()

    prepare_q(0)
    start_q(0)
    for c in range(1, CHUNKS):
        prepare_q(c)

    row_at = lax.broadcasted_iota(jnp.int32, (rows, LANES), 0)
    lane_at = lax.broadcasted_iota(jnp.int32, (rows, LANES), 1)
    ids = jnp.concatenate([
        jnp.transpose(jnp.broadcast_to(ids_ref[:, i * LANES:(i + 1) * LANES], (LANES, LANES)))
        for i in range(id_rows)
    ])
    for chunk in range((REACH + 1) * id_rows):
        key_ids = meta_all[pl.ds(me + chunk // id_rows, 1)][0, chunk % id_rows:chunk % id_rows + 1, :]
        key_at = lane_at + (chunk * LANES - REACH * rows)
        bias[:, chunk * LANES:(chunk + 1) * LANES] = jnp.where(
            (ids == key_ids) & (key_at <= row_at), 0.0, MASKED
        )

    for d, distance, rank, sends, receives in routes:
        @pl.when(receives)
        def _():
            remote(send_kv.at[d], recv_kv.at[d], kv_send.at[d], kv_recv.at[d], rank).wait_recv()

    def source(slot):
        block = me * recv + slot
        return block < offset, block >= offset + count

    for slot in range(recv):
        before, after = source(slot)
        at = pl.ds(slot * BLOCK, BLOCK)
        home = pl.ds((4 + core) * rows + slot * BLOCK, BLOCK)
        chosen = pick(0, slot)
        for part_at, held in ((0, kv), (1, vv)):
            columns = slice(part_at * kv_width, (part_at + 1) * kv_width)
            own = held[chosen]
            got = jnp.where(before, recv_kv[0, at, columns], own)
            got = jnp.where(after, recv_kv[1, at, columns], got)
            for g in range(KV_HEADS):
                win[g, home, part_at * D_HEAD:(part_at + 1) * D_HEAD] = got[
                    :, g * D_HEAD:(g + 1) * D_HEAD
                ]

    def win_copy(hop, g, place, rank):
        here = win.at[g, pl.ds((place + core) * rows, rows), :]
        dst = place - hop if hop in (2, 4) else place
        there = win.at[g, pl.ds((dst + core) * rows, rows), :]
        index = {2: 0, 4: 1}.get(hop, 2 + place // 2)
        return remote(here, there, win_send.at[index, g], win_recv.at[index, g], rank)

    def start_win(g):
        for hop in (2, 4):
            @pl.when(me + hop < n)
            def _():
                win_copy(hop, g, 4, me + hop).start()
        win_copy(0, g, 4, partner).start()

    def forward_win(g):
        for hop in (2, 4):
            @pl.when(me >= hop)
            def _():
                win_copy(hop, g, 4, me + hop).wait_recv()
                win_copy(0, g, 4 - hop, partner).start()

    start_win(0)
    start_q(1)
    start_q(2)
    start_q(3)
    forward_q(0)
    start_win(1)
    start_q(4)
    start_q(5)
    forward_win(0)
    forward_q(1)
    for c in range(6, AHEAD):
        start_q(c)
    for c in range(2, LEAD):
        forward_q(c)

    span = (REACH + 1) * rows - (recv - 1) * BLOCK
    scale = D_HEAD ** -0.5 * LOG2E

    def out_copy(c):
        columns = pl.ds(c * width, width)
        return pltpu.make_async_copy(out_buf.at[:, columns], out_ref.at[:, columns], out_sem.at[c])

    for c in range(CHUNKS):
        g = c * PER_CHUNK // PER_GROUP
        opens = c * PER_CHUNK % PER_GROUP == 0
        for d, distance, rank, sends, receives in routes:
            @pl.when(receives)
            def _():
                q_copy(d, c, rank).wait_recv()
        if c + AHEAD < CHUNKS:
            start_q(c + AHEAD)
        for slot in range(recv):
            before, after = source(slot)
            at = pl.ds(slot * BLOCK, BLOCK)
            chosen = pick(0, slot)
            for h in range(PER_CHUNK):
                columns = slice(h * D_HEAD, (h + 1) * D_HEAD)
                own = qv[chosen, :, c * width + h * D_HEAD:c * width + (h + 1) * D_HEAD]
                got = jnp.where(before, recv_q[0, c, at, columns], own)
                got = jnp.where(after, recv_q[1, c, at, columns], got)
                qp[h, at, :] = got
        if opens:
            win_copy(0, g, 4, partner).wait_recv()
            for hop in (2, 4):
                @pl.when(me >= hop)
                def _():
                    win_copy(0, g, 4 - hop, partner).wait_recv()

        for slot in range(recv):
            if slot == 1 and c + LEAD < CHUNKS:
                forward_q(c + LEAD)
            start = pl.multiple_of(core * rows + slot * BLOCK, BLOCK)
            at = slice(slot * BLOCK, (slot + 1) * BLOCK)
            keys = win.at[g, pl.ds(start, span), :D_HEAD]
            values = win.at[g, pl.ds(start, span), D_HEAD:]
            for pair in range(PER_CHUNK // 2):
                query = qp[pair * 2:pair * 2 + 2, at, :].reshape(2 * BLOCK, D_HEAD)
                logits = lax.dot_general(
                    query, keys[...], (((1,), (1,)), ((), ())),
                    preferred_element_type=jnp.float32,
                )
                mask = bias[at, slot * BLOCK:slot * BLOCK + span]
                logits = logits.reshape(2, BLOCK, span) * scale + mask[None]
                top = jnp.max(logits, axis=-1, keepdims=True)
                raised = jnp.exp2(logits - top)
                totals = jnp.sum(raised, axis=-1, keepdims=True)
                weights = raised.astype(jnp.bfloat16).reshape(2 * BLOCK, span)
                head_out = jnp.dot(weights, values[...], preferred_element_type=jnp.float32)
                head_out = (head_out.reshape(2, BLOCK, D_HEAD) / totals).astype(jnp.bfloat16)
                for i in range(2):
                    head = c * PER_CHUNK + pair * 2 + i
                    out_buf[at, head * D_HEAD:(head + 1) * D_HEAD] = head_out[i]
                    score[at, :] += head_out[i].astype(jnp.float32) * dir_ref[head:head + 1, :]

        out_copy(c).start()
        if opens and g + 1 < KV_HEADS:
            forward_win(g + 1)
            if g + 2 < KV_HEADS:
                start_win(g + 2)

    next_first = meta_all[pl.ds(me + REACH + 1, 1)][0, 0:1, 0:1]
    following = jnp.where(row_at == rows - 1, next_first, pltpu.roll(ids, rows - 1, 0))
    token_score = jnp.sum(score[...], axis=-1, keepdims=True)
    chosen = (ids == lane_at) & (ids != following)
    partial = jnp.sum(jnp.where(chosen, token_score, 0.0), axis=0, keepdims=True)
    part[...] = jnp.broadcast_to(partial, part.shape)
    part_all[pl.ds(me, 1)] = part[...][None]
    tell_all(part, part_all, 0, part_send, part_recv)

    for d, distance, rank, sends, receives in routes:
        @pl.when(sends)
        def _():
            remote(send_kv.at[d], recv_kv.at[d], kv_send.at[d], kv_recv.at[d], rank).wait_send()
            for c in range(CHUNKS):
                q_copy(d, c, rank).wait_send()
    for g in range(KV_HEADS):
        win_copy(0, g, 4, partner).wait_send()
        for hop in (2, 4):
            @pl.when(me + hop < n)
            def _():
                win_copy(hop, g, 4, me + hop).wait_send()

            @pl.when(me >= hop)
            def _():
                win_copy(0, g, 4 - hop, partner).wait_send()

    for c in range(CHUNKS):
        @pl.when(relays(c))
        def _():
            relay_on(c).wait_send()

        out_copy(c).wait()
    hear_all(part, part_all, 0, part_send, part_recv)
    rew_ref[...] = jnp.sum(part_all[...], axis=0)[0:1, :rew_ref.shape[1]]


def handed_on(source, target, held, in_sem, out_sem):
    step = source.shape[0] // PARTS
    parts = [pl.ds(i * step, step) for i in range(PARTS)]
    reads = [
        pltpu.make_async_copy(source.at[at], held.at[at], in_sem.at[i])
        for i, at in enumerate(parts)
    ]
    writes = [
        pltpu.make_async_copy(held.at[at], target.at[at], out_sem.at[i])
        for i, at in enumerate(parts)
    ]
    for read in reads:
        read.start()
    for read, write in zip(reads, writes):
        read.wait()
        write.start()
    for write in writes:
        write.wait()


def shards(queries, keys, values, block_counts, segment_ids, reward_dir):
    n = lax.axis_size("dp")
    rows = segment_ids.shape[0]
    cap = queries.shape[0] // BLOCK
    kv_width = keys.shape[1]
    width = PER_CHUNK * D_HEAD
    response_count = n * 2 // REACH
    vmem = pl.BlockSpec(memory_space=pltpu.VMEM)
    hbm = pl.BlockSpec(memory_space=pl.ANY)
    dma = pltpu.SemaphoreType.DMA
    bf16 = jnp.bfloat16
    attn_out, rewards = pl.pallas_call(
        functools.partial(kernel, n),
        out_shape=(
            jax.ShapeDtypeStruct((rows, HEADS * D_HEAD), bf16),
            jax.ShapeDtypeStruct((1, response_count), jnp.float32),
        ),
        in_specs=[hbm, hbm, hbm, pl.BlockSpec(memory_space=pltpu.SMEM), vmem, vmem],
        out_specs=(hbm, vmem),
        scratch_shapes=[
            pltpu.VMEM((8, LANES), jnp.int32),
            pltpu.VMEM((cap, BLOCK, HEADS * D_HEAD), bf16),
            pltpu.VMEM((cap, BLOCK, kv_width), bf16),
            pltpu.VMEM((cap, BLOCK, kv_width), bf16),
            pltpu.VMEM((n + REACH + 1, 8, LANES), jnp.int32),
            pltpu.VMEM((2, CHUNKS, rows, width), bf16),
            pltpu.VMEM((2, CHUNKS, rows, width), bf16),
            pltpu.VMEM((2, rows, 2 * kv_width), bf16),
            pltpu.VMEM((2, rows, 2 * kv_width), bf16),
            pltpu.VMEM((KV_HEADS, (REACH + 2) * rows, 2 * D_HEAD), bf16),
            pltpu.VMEM((PER_CHUNK, rows, D_HEAD), bf16),
            pltpu.VMEM((rows, (REACH + 1) * rows), jnp.float32),
            pltpu.VMEM((rows, LANES), jnp.float32),
            pltpu.VMEM((8, LANES), jnp.float32),
            pltpu.VMEM((n, 8, LANES), jnp.float32),
            pltpu.VMEM((CHUNKS, rows, width), bf16),
            pltpu.VMEM((rows, HEADS * D_HEAD), bf16),
            dma((3,)),
            dma((n,)), dma((n,)),
            dma((2,)), dma((2,)),
            dma((2, CHUNKS)), dma((2, CHUNKS)),
            dma((5, KV_HEADS)), dma((5, KV_HEADS)),
            dma((n,)), dma((n,)),
            dma((CHUNKS,)), dma((CHUNKS,)), dma((CHUNKS,)),
        ],
        compiler_params=pltpu.CompilerParams(
            collective_id=0, has_side_effects=True, vmem_limit_bytes=56 * 1024 * 1024
        ),
    )(
        queries.reshape(cap, BLOCK, -1), keys.reshape(cap, BLOCK, -1),
        values.reshape(cap, BLOCK, -1), block_counts, segment_ids.reshape(1, rows), reward_dir.reshape(HEADS, D_HEAD),
    )
    attn_out = pl.pallas_call(
        handed_on,
        out_shape=jax.ShapeDtypeStruct(attn_out.shape, bf16),
        in_specs=[hbm],
        out_specs=hbm,
        scratch_shapes=[pltpu.VMEM(attn_out.shape, bf16), dma((PARTS,)), dma((PARTS,))],
        compiler_params=pltpu.CompilerParams(vmem_limit_bytes=56 * 1024 * 1024),
    )(attn_out)
    return attn_out, rewards.reshape(response_count)


def solution(mesh):
    return jax.shard_map(
        shards,
        mesh=mesh,
        in_specs=(
            P(("groups", "dp"), None),
            P(("groups", "dp"), None),
            P(("groups", "dp"), None),
            P(("groups", "dp")),
            P(("groups", "dp")),
            P(),
        ),
        out_specs=(P(("groups", "dp"), None), P("groups")),
        check_vma=False,
    )
```

```python
import functools

import jax
import jax.numpy as jnp
from jax import lax
from jax.experimental import pallas as pl
from jax.experimental.pallas import tpu as pltpu
from jax.sharding import PartitionSpec as P

D_HEAD = 128
HEADS = 32
KV_HEADS = 4
BLOCK = 128
REACH = 4
LANES = 128
PER_GROUP = HEADS // KV_HEADS
PER_CHUNK = 4
CHUNKS = HEADS // PER_CHUNK
AHEAD = 4
LEAD = 2
PARTS = 8
PLANE = 4
LOG2E = 1.4426950408889634
MASKED = -1e30


def kernel(
    n, q_hbm, k_hbm, v_hbm, count_ref, ids_ref, dir_ref, out_ref, rew_ref,
    meta_ref, qv, kv, vv, meta_all, send_q, recv_q, send_kv, recv_kv, win, qp, bias, score,
    part, part_all, relay, out_buf,
    load_sem, meta_send, meta_recv, kv_send, kv_recv, q_send, q_recv,
    win_send, win_recv, part_send, part_recv, relay_send, relay_recv, out_sem,
):
    me = lax.axis_index("dp")
    core = lax.rem(me, 2)
    partner = me + 1 - 2 * core
    rows = ids_ref.shape[1]
    recv = rows // BLOCK
    cap = qv.shape[0]
    width = PER_CHUNK * D_HEAD
    kv_width = KV_HEADS * D_HEAD
    id_rows = rows // LANES

    loads = [
        pltpu.make_async_copy(k_hbm, kv, load_sem.at[0]),
        pltpu.make_async_copy(v_hbm, vv, load_sem.at[1]),
        pltpu.make_async_copy(q_hbm, qv, load_sem.at[2]),
    ]
    for load in loads:
        load.start()

    count = count_ref[0]
    meta_ref[...] = jnp.full((8, LANES), count, jnp.int32)
    for i in range(id_rows):
        meta_ref[i:i + 1, :] = ids_ref[:, i * LANES:(i + 1) * LANES]
    for pad in list(range(REACH)) + [n + REACH]:
        meta_all[pad] = jnp.full((8, LANES), -1, jnp.int32)
    meta_all[pl.ds(me + REACH, 1)] = meta_ref[...][None]
    for distance in (2, 4):
        @pl.when(me < distance)
        def _():
            win[:, pl.ds((4 - distance) * rows, 2 * rows), :] = jnp.zeros(
                (KV_HEADS, 2 * rows, 2 * D_HEAD), win.dtype
            )
    score[...] = jnp.zeros_like(score)

    barrier = pltpu.get_barrier_semaphore()

    def greet(i, carry):
        pl.semaphore_signal(
            barrier, inc=1, device_id={"dp": lax.rem(me + i, n)},
            device_id_type=pl.DeviceIdType.MESH,
        )
        return carry

    lax.fori_loop(1, n, greet, 0)
    pl.semaphore_wait(barrier, n - 1)

    def remote(src, dst, send_sem, recv_sem, rank):
        return pltpu.make_async_remote_copy(
            src_ref=src, dst_ref=dst, send_sem=send_sem, recv_sem=recv_sem,
            device_id={"dp": rank}, device_id_type=pl.DeviceIdType.MESH,
        )

    def tell_all(src, table, shift, send_sem, recv_sem):
        def begin(i, carry):
            remote(src, table.at[me + shift], send_sem.at[i], recv_sem.at[i],
                   lax.rem(me + i, n)).start()
            return carry

        lax.fori_loop(1, n, begin, 0)

    def hear_all(src, table, shift, send_sem, recv_sem):
        def finish(i, carry):
            came = lax.rem(me + n - i, n)
            remote(src, table.at[came + shift], send_sem.at[i], recv_sem.at[i],
                   lax.rem(me + i, n)).wait()
            return carry

        lax.fori_loop(1, n, finish, 0)

    tell_all(meta_ref, meta_all, REACH, meta_send, meta_recv)
    hear_all(meta_ref, meta_all, REACH, meta_send, meta_recv)

    counts = meta_all[REACH:REACH + n, id_rows, :]
    rank_index = lax.broadcasted_iota(jnp.int32, (n, LANES), 0)
    offset = jnp.sum(jnp.where(rank_index < me, counts, 0), axis=0, keepdims=True)[0, 0]

    def pick(distance, slot):
        return jnp.clip((me + distance) * recv + slot - offset, 0, cap - 1)

    routes = ((0, 1, me + 1, me < n - 1, me > 0), (1, -1, me - 1, me > 0, me < n - 1))

    def both(start_or_wait):
        for d, distance, rank, sends, receives in routes:
            start_or_wait(d, rank, sends, receives)

    for load in loads[:2]:
        load.wait()
    for d, distance, rank, sends, receives in routes:
        for slot in range(recv):
            at = pl.ds(slot * BLOCK, BLOCK)
            chosen = pick(distance, slot)
            send_kv[d, at, :kv_width] = kv[chosen]
            send_kv[d, at, kv_width:] = vv[chosen]

        @pl.when(sends)
        def _():
            remote(send_kv.at[d], recv_kv.at[d], kv_send.at[d], kv_recv.at[d], rank).start()

    loads[2].wait()

    def prepare_q(g):
        for d, distance, rank, sends, receives in routes:
            for slot in range(recv):
                send_q[d, g, pl.ds(slot * BLOCK, BLOCK), :] = qv[
                    pick(distance, slot), :, g * width:(g + 1) * width
                ]

    def q_copy(d, g, rank):
        return remote(send_q.at[d, g], recv_q.at[d, g], q_send.at[d, g], q_recv.at[d, g], rank)

    place = lax.rem(me, PLANE)
    plane = me // PLANE
    planes = n // PLANE

    def early(border, c):
        return (c * 3 % CHUNKS) * planes < (planes - 1 - border) * CHUNKS

    def crosses(d):
        return place == (PLANE - 1 if d == 0 else 0)

    def relay_out(d, c):
        border = plane if d == 0 else plane - 1
        near, far = (-2, 4) if d == 0 else (-4, 2)
        rank = jnp.where(early(border, c), me + near, me + far)
        return remote(send_q.at[d, c], relay.at[c], q_send.at[d, c], relay_recv.at[c], rank)

    relay_d = 1 - lax.rem(place, 2)
    relay_to = jnp.where(place < 2, me + 3, me - 3)
    relay_border = jnp.where(place < 2, plane, plane - 1)
    relay_open = (relay_border >= 0) & (relay_border < planes - 1)

    def relays(c):
        return relay_open & (early(relay_border, c) == (place < 2))

    def relay_on(c):
        return remote(
            relay.at[c], recv_q.at[relay_d, c], relay_send.at[c], q_recv.at[relay_d, c], relay_to
        )

    def forward_q(c):
        @pl.when(relays(c))
        def _():
            remote(relay.at[c], relay.at[c], relay_send.at[c], relay_recv.at[c], relay_to).wait_recv()
            relay_on(c).start()

    def start_q(g):
        for d, distance, rank, sends, receives in routes:
            @pl.when(sends & crosses(d))
            def _():
                relay_out(d, g).start()

            @pl.when(sends & jnp.logical_not(crosses(d)))
            def _():
                q_copy(d, g, rank).start()

    prepare_q(0)
    start_q(0)
    for c in range(1, CHUNKS):
        prepare_q(c)

    row_at = lax.broadcasted_iota(jnp.int32, (rows, LANES), 0)
    lane_at = lax.broadcasted_iota(jnp.int32, (rows, LANES), 1)
    ids = jnp.concatenate([
        jnp.transpose(jnp.broadcast_to(ids_ref[:, i * LANES:(i + 1) * LANES], (LANES, LANES)))
        for i in range(id_rows)
    ])
    for chunk in range((REACH + 1) * id_rows):
        key_ids = meta_all[pl.ds(me + chunk // id_rows, 1)][0, chunk % id_rows:chunk % id_rows + 1, :]
        key_at = lane_at + (chunk * LANES - REACH * rows)
        bias[:, chunk * LANES:(chunk + 1) * LANES] = jnp.where(
            (ids == key_ids) & (key_at <= row_at), 0.0, MASKED
        )

    for d, distance, rank, sends, receives in routes:
        @pl.when(receives)
        def _():
            remote(send_kv.at[d], recv_kv.at[d], kv_send.at[d], kv_recv.at[d], rank).wait_recv()

    def source(slot):
        block = me * recv + slot
        return block < offset, block >= offset + count

    for slot in range(recv):
        before, after = source(slot)
        at = pl.ds(slot * BLOCK, BLOCK)
        home = pl.ds((4 + core) * rows + slot * BLOCK, BLOCK)
        chosen = pick(0, slot)
        for part_at, held in ((0, kv), (1, vv)):
            columns = slice(part_at * kv_width, (part_at + 1) * kv_width)
            own = held[chosen]
            got = jnp.where(before, recv_kv[0, at, columns], own)
            got = jnp.where(after, recv_kv[1, at, columns], got)
            for g in range(KV_HEADS):
                win[g, home, part_at * D_HEAD:(part_at + 1) * D_HEAD] = got[
                    :, g * D_HEAD:(g + 1) * D_HEAD
                ]

    def win_copy(hop, g, place, rank):
        here = win.at[g, pl.ds((place + core) * rows, rows), :]
        dst = place - hop if hop in (2, 4) else place
        there = win.at[g, pl.ds((dst + core) * rows, rows), :]
        index = {2: 0, 4: 1}.get(hop, 2 + place // 2)
        return remote(here, there, win_send.at[index, g], win_recv.at[index, g], rank)

    def start_win(g):
        for hop in (2, 4):
            @pl.when(me + hop < n)
            def _():
                win_copy(hop, g, 4, me + hop).start()
        win_copy(0, g, 4, partner).start()

    def forward_win(g):
        for hop in (2, 4):
            @pl.when(me >= hop)
            def _():
                win_copy(hop, g, 4, me + hop).wait_recv()
                win_copy(0, g, 4 - hop, partner).start()

    start_win(0)
    start_q(1)
    forward_q(0)
    start_win(1)
    start_q(2)
    forward_win(0)
    start_q(3)
    forward_q(1)

    span = (REACH + 1) * rows - (recv - 1) * BLOCK
    scale = D_HEAD ** -0.5 * LOG2E

    def out_copy(c):
        columns = pl.ds(c * width, width)
        return pltpu.make_async_copy(out_buf.at[:, columns], out_ref.at[:, columns], out_sem.at[c])

    for c in range(CHUNKS):
        g = c * PER_CHUNK // PER_GROUP
        opens = c * PER_CHUNK % PER_GROUP == 0
        for d, distance, rank, sends, receives in routes:
            @pl.when(receives)
            def _():
                q_copy(d, c, rank).wait_recv()
        if c + AHEAD < CHUNKS:
            start_q(c + AHEAD)
        for slot in range(recv):
            before, after = source(slot)
            at = pl.ds(slot * BLOCK, BLOCK)
            chosen = pick(0, slot)
            for h in range(PER_CHUNK):
                columns = slice(h * D_HEAD, (h + 1) * D_HEAD)
                own = qv[chosen, :, c * width + h * D_HEAD:c * width + (h + 1) * D_HEAD]
                got = jnp.where(before, recv_q[0, c, at, columns], own)
                got = jnp.where(after, recv_q[1, c, at, columns], got)
                qp[h, at, :] = got
        if opens:
            win_copy(0, g, 4, partner).wait_recv()
            for hop in (2, 4):
                @pl.when(me >= hop)
                def _():
                    win_copy(0, g, 4 - hop, partner).wait_recv()

        for slot in range(recv):
            if slot == 1 and c + LEAD < CHUNKS:
                forward_q(c + LEAD)
            start = pl.multiple_of(core * rows + slot * BLOCK, BLOCK)
            at = slice(slot * BLOCK, (slot + 1) * BLOCK)
            keys = win.at[g, pl.ds(start, span), :D_HEAD]
            values = win.at[g, pl.ds(start, span), D_HEAD:]
            for pair in range(PER_CHUNK // 2):
                query = qp[pair * 2:pair * 2 + 2, at, :].reshape(2 * BLOCK, D_HEAD)
                logits = lax.dot_general(
                    query, keys[...], (((1,), (1,)), ((), ())),
                    preferred_element_type=jnp.float32,
                )
                mask = bias[at, slot * BLOCK:slot * BLOCK + span]
                logits = logits.reshape(2, BLOCK, span) * scale + mask[None]
                top = jnp.max(logits, axis=-1, keepdims=True)
                raised = jnp.exp2(logits - top)
                totals = jnp.sum(raised, axis=-1, keepdims=True)
                weights = raised.astype(jnp.bfloat16).reshape(2 * BLOCK, span)
                head_out = jnp.dot(weights, values[...], preferred_element_type=jnp.float32)
                head_out = (head_out.reshape(2, BLOCK, D_HEAD) / totals).astype(jnp.bfloat16)
                for i in range(2):
                    head = c * PER_CHUNK + pair * 2 + i
                    out_buf[at, head * D_HEAD:(head + 1) * D_HEAD] = head_out[i]
                    score[at, :] += head_out[i].astype(jnp.float32) * dir_ref[head:head + 1, :]

        out_copy(c).start()
        if opens and g + 1 < KV_HEADS:
            forward_win(g + 1)
            if g + 2 < KV_HEADS:
                start_win(g + 2)

    next_first = meta_all[pl.ds(me + REACH + 1, 1)][0, 0:1, 0:1]
    following = jnp.where(row_at == rows - 1, next_first, pltpu.roll(ids, rows - 1, 0))
    token_score = jnp.sum(score[...], axis=-1, keepdims=True)
    chosen = (ids == lane_at) & (ids != following)
    partial = jnp.sum(jnp.where(chosen, token_score, 0.0), axis=0, keepdims=True)
    part[...] = jnp.broadcast_to(partial, part.shape)
    part_all[pl.ds(me, 1)] = part[...][None]
    tell_all(part, part_all, 0, part_send, part_recv)

    for d, distance, rank, sends, receives in routes:
        @pl.when(sends)
        def _():
            remote(send_kv.at[d], recv_kv.at[d], kv_send.at[d], kv_recv.at[d], rank).wait_send()
            for c in range(CHUNKS):
                q_copy(d, c, rank).wait_send()
    for g in range(KV_HEADS):
        win_copy(0, g, 4, partner).wait_send()
        for hop in (2, 4):
            @pl.when(me + hop < n)
            def _():
                win_copy(hop, g, 4, me + hop).wait_send()

            @pl.when(me >= hop)
            def _():
                win_copy(0, g, 4 - hop, partner).wait_send()

    for c in range(CHUNKS):
        @pl.when(relays(c))
        def _():
            relay_on(c).wait_send()

        out_copy(c).wait()
    hear_all(part, part_all, 0, part_send, part_recv)
    rew_ref[...] = jnp.sum(part_all[...], axis=0)[0:1, :rew_ref.shape[1]]


def handed_on(source, target, held, in_sem, out_sem):
    step = source.shape[0] // PARTS
    parts = [pl.ds(i * step, step) for i in range(PARTS)]
    reads = [
        pltpu.make_async_copy(source.at[at], held.at[at], in_sem.at[i])
        for i, at in enumerate(parts)
    ]
    writes = [
        pltpu.make_async_copy(held.at[at], target.at[at], out_sem.at[i])
        for i, at in enumerate(parts)
    ]
    for read in reads:
        read.start()
    for read, write in zip(reads, writes):
        read.wait()
        write.start()
    for write in writes:
        write.wait()


def shards(queries, keys, values, block_counts, segment_ids, reward_dir):
    n = lax.axis_size("dp")
    rows = segment_ids.shape[0]
    cap = queries.shape[0] // BLOCK
    kv_width = keys.shape[1]
    width = PER_CHUNK * D_HEAD
    response_count = n * 2 // REACH
    vmem = pl.BlockSpec(memory_space=pltpu.VMEM)
    hbm = pl.BlockSpec(memory_space=pl.ANY)
    dma = pltpu.SemaphoreType.DMA
    bf16 = jnp.bfloat16
    attn_out, rewards = pl.pallas_call(
        functools.partial(kernel, n),
        out_shape=(
            jax.ShapeDtypeStruct((rows, HEADS * D_HEAD), bf16),
            jax.ShapeDtypeStruct((1, response_count), jnp.float32),
        ),
        in_specs=[hbm, hbm, hbm, pl.BlockSpec(memory_space=pltpu.SMEM), vmem, vmem],
        out_specs=(hbm, vmem),
        scratch_shapes=[
            pltpu.VMEM((8, LANES), jnp.int32),
            pltpu.VMEM((cap, BLOCK, HEADS * D_HEAD), bf16),
            pltpu.VMEM((cap, BLOCK, kv_width), bf16),
            pltpu.VMEM((cap, BLOCK, kv_width), bf16),
            pltpu.VMEM((n + REACH + 1, 8, LANES), jnp.int32),
            pltpu.VMEM((2, CHUNKS, rows, width), bf16),
            pltpu.VMEM((2, CHUNKS, rows, width), bf16),
            pltpu.VMEM((2, rows, 2 * kv_width), bf16),
            pltpu.VMEM((2, rows, 2 * kv_width), bf16),
            pltpu.VMEM((KV_HEADS, (REACH + 2) * rows, 2 * D_HEAD), bf16),
            pltpu.VMEM((PER_CHUNK, rows, D_HEAD), bf16),
            pltpu.VMEM((rows, (REACH + 1) * rows), jnp.float32),
            pltpu.VMEM((rows, LANES), jnp.float32),
            pltpu.VMEM((8, LANES), jnp.float32),
            pltpu.VMEM((n, 8, LANES), jnp.float32),
            pltpu.VMEM((CHUNKS, rows, width), bf16),
            pltpu.VMEM((rows, HEADS * D_HEAD), bf16),
            dma((3,)),
            dma((n,)), dma((n,)),
            dma((2,)), dma((2,)),
            dma((2, CHUNKS)), dma((2, CHUNKS)),
            dma((5, KV_HEADS)), dma((5, KV_HEADS)),
            dma((n,)), dma((n,)),
            dma((CHUNKS,)), dma((CHUNKS,)), dma((CHUNKS,)),
        ],
        compiler_params=pltpu.CompilerParams(
            collective_id=0, has_side_effects=True, vmem_limit_bytes=56 * 1024 * 1024
        ),
    )(
        queries.reshape(cap, BLOCK, -1), keys.reshape(cap, BLOCK, -1),
        values.reshape(cap, BLOCK, -1), block_counts, segment_ids.reshape(1, rows), reward_dir.reshape(HEADS, D_HEAD),
    )
    attn_out = pl.pallas_call(
        handed_on,
        out_shape=jax.ShapeDtypeStruct(attn_out.shape, bf16),
        in_specs=[hbm],
        out_specs=hbm,
        scratch_shapes=[pltpu.VMEM(attn_out.shape, bf16), dma((PARTS,)), dma((PARTS,))],
        compiler_params=pltpu.CompilerParams(vmem_limit_bytes=56 * 1024 * 1024),
    )(attn_out)
    return attn_out, rewards.reshape(response_count)


def solution(mesh):
    return jax.shard_map(
        shards,
        mesh=mesh,
        in_specs=(
            P(("groups", "dp"), None),
            P(("groups", "dp"), None),
            P(("groups", "dp"), None),
            P(("groups", "dp")),
            P(("groups", "dp")),
            P(),
        ),
        out_specs=(P(("groups", "dp"), None), P("groups")),
        check_vma=False,
    )
```
